256 devices in a mesh: tm: 32 (over z_lo, x, core), op: 8 (over y, z_hi).
Axes of the slice: x: 4, y: 4, z: 8 (z_hi: 2, z_lo: 4; z = z_hi * 4 + z_lo), core: 2. Of those that a mesh axis runs over, the one named last changes fastest.
Arguments:
- peram: bfloat16 [32, 2, 256, 256], P('tm'), may hold values from -0.375 to 0.375
- sink_elementals: bfloat16 [32, 96, 2, 256, 256], P('tm', 'op'), may hold values from -0.375 to 0.375
- source_elementals: bfloat16 [96, 2, 256, 256], P('tm', None, 'op'), may hold values from -0.375 to 0.375
- irrep: int32 [96], replicated, may hold values from 0 to 3
Outputs:
- corr: float32 [32, 2, 96, 96], P('tm', None, 'op')
The draws below stay inside these ranges and needn't reach their ends.
All inputs are finite; a program needn't handle non-finite values.
Results may differ from the reference program's by a relative error of at most 0.0041.
Values may be sent and summed in bfloat16 or wider, within the bound.
A program may use at most 128 MiB of HBM per device.

```python
import jax
import jax.numpy as jnp
from jax import lax

NVEC = 64
SPIN_EIGEN_DIM = 256
MESON_OPERATORS = 96
NIRREP = 4
SINK_SLICES = 32


def with_ends(array, rng, least, largest):
    spot = [jax.random.randint(jax.random.fold_in(rng, axis), (), 0, length) for axis, length in enumerate(array.shape)]
    main_axis = array.shape.index(max(array.shape))
    beside = spot[:main_axis] + [(spot[main_axis] + 1) % array.shape[main_axis]] + spot[main_axis + 1:]
    return array.at[tuple(spot)].set(least).at[tuple(beside)].set(largest)


def level_of(stream_key, shape, pieces, low, high):
    loudness, own = 1.0, jax.random.fold_in(stream_key, 6)
    for axis_at, shards_of in pieces:
        steps = jnp.exp(jax.random.uniform(jax.random.fold_in(own, axis_at), (shards_of,), jnp.float32, low / len(pieces), high / len(pieces)))
        loudness = loudness * jnp.repeat(steps, shape[axis_at] // shards_of).reshape([-1 if axis == axis_at else 1 for axis in range(len(shape))])
    return loudness


def normal_values(stream_key, extent, width, bound, split=(), kind=jnp.bfloat16):
    drawn = jax.random.normal(stream_key, extent, jnp.float32) * width
    if len(split) > 0:
        drawn = level_of(stream_key, extent, split, -0.22, 0.18) * drawn
    return jnp.clip(drawn, min=-bound, max=bound).astype(kind)


def setup_inputs(seed: int = 0) -> dict:
    arg_keys = jax.random.split(jax.random.key(seed), 5)
    peram = normal_values(arg_keys[0], (SINK_SLICES, 2, SPIN_EIGEN_DIM, SPIN_EIGEN_DIM), SPIN_EIGEN_DIM ** -0.5, 0.375, ((0, 32),))
    sink_elementals = normal_values(arg_keys[1], (SINK_SLICES, MESON_OPERATORS, 2, SPIN_EIGEN_DIM, SPIN_EIGEN_DIM), SPIN_EIGEN_DIM ** -0.5, 0.375, ((0, 32), (1, 8)))
    source_elementals = normal_values(arg_keys[2], (MESON_OPERATORS, 2, SPIN_EIGEN_DIM, SPIN_EIGEN_DIM), SPIN_EIGEN_DIM ** -0.5, 0.375, ((0, 32), (2, 8)))
    irrep = with_ends(jax.random.randint(arg_keys[3], (MESON_OPERATORS,), 0, NIRREP), jax.random.fold_in(arg_keys[3], 1), 0, NIRREP - 1).astype(jnp.int32)
    return dict(peram=peram, sink_elementals=sink_elementals, source_elementals=source_elementals, irrep=irrep)


def spin_signs():
    slice_index = jnp.arange(SPIN_EIGEN_DIM)
    return jnp.where(slice_index < 2 * NVEC, 1.0, -1.0).astype(jnp.float32)


def to_bf(value):
    return value.astype(jnp.bfloat16).astype(jnp.float32)


def reference(peram, sink_elementals, source_elementals, irrep):
    signs = spin_signs()
    both = signs[:, None] * signs[None, :]
    src_re = source_elementals[:, 0].astype(jnp.float32)
    src_im = source_elementals[:, 1].astype(jnp.float32)

    def one_time(packed):
        tau, elem = packed
        tau_re = tau[0].astype(jnp.float32)
        tau_im = tau[1].astype(jnp.float32)
        bar_re = both * tau_re
        barred_imaginary = -(both * tau_im)
        el_re = elem[:, 0].astype(jnp.float32)
        el_im = elem[:, 1].astype(jnp.float32)
        prod_re = jnp.einsum('ocd,de->oce', el_re, tau_re) - jnp.einsum('ocd,de->oce', el_im, tau_im)
        prod_im = jnp.einsum('ocd,de->oce', el_re, tau_im) + jnp.einsum('ocd,de->oce', el_im, tau_re)
        prod_re = to_bf(prod_re)
        prod_im = to_bf(prod_im)
        turn_re = jnp.einsum('ocb,ca->oba', prod_re, bar_re) - jnp.einsum('ocb,ca->oba', prod_im, barred_imaginary)
        turn_im = jnp.einsum('ocb,ca->oba', prod_re, barred_imaginary) + jnp.einsum('ocb,ca->oba', prod_im, bar_re)
        turn_re = to_bf(turn_re)
        turn_im = to_bf(turn_im)
        full_re = jnp.einsum('oba,jba->oj', turn_re, src_re) - jnp.einsum('oba,jba->oj', turn_im, src_im)
        complete_imaginary = jnp.einsum('oba,jba->oj', turn_re, src_im) + jnp.einsum('oba,jba->oj', turn_im, src_re)
        return jnp.stack([full_re, complete_imaginary], axis=0)

    full = lax.map(one_time, (peram, sink_elementals))
    same = (irrep[:, None] == irrep[None, :]).astype(jnp.float32)
    return full * same[None, None, :, :]
```

```python
import jax
import jax.numpy as jnp
from jax import lax
from jax.experimental import pallas as pl
from jax.experimental.pallas import tpu as pltpu
from jax.sharding import PartitionSpec as P

MESH = pl.DeviceIdType.MESH
BF = jnp.bfloat16
F32 = jnp.float32
GROUPS = 3
STRIDE_T = 128
STRIDE_S = 48

HOPS = (
    ((0, 0), (0, 0)),
    ((1, 0), (1, 0)),
    ((3, 0), (3, 0)),
    ((0, 1), (0, 1)),
    ((0, 3), (0, 3)),
    ((3, 3), (3, 3)),
    ((1, 3), (3, 1)),
    ((2, 0), (0, 2)),
)


def dot_t(a, b):
    return lax.dot_general(a, b, (((1,), (1,)), ((), ())), preferred_element_type=F32)


def kernel(
    peram_ref, sink_ref, src_ref, out_ref,
    per_v, sink_v, src_v, left, bar, tout, recv, sring, fs, ft, sw, oret, ogot,
    in_sem, sink_sem, s1_send, s1_recv, ring_send, ring_recv, t_send, t_recv, o_send, o_recv,
):
    tm = lax.axis_index("tm")
    op = lax.axis_index("op")
    core = tm % 2
    x = (tm // 2) % 4
    y = op // 2
    z = (op % 2) * 4 + tm // 8

    def dev(x_, y_, z_, c_):
        return ((z_ % 4) * 8 + x_ * 2 + c_, y_ * 2 + z_ // 4)

    def block_of(x_, y_):
        p = (x_ + 4 - y_) % 4
        return y_ % 2 + 2 * (p // 2), p % 2

    cp_src = pltpu.make_async_copy(src_ref, src_v, in_sem.at[0])
    cp_per = pltpu.make_async_copy(peram_ref.at[0], per_v, in_sem.at[1])
    cp_src.start()
    cp_per.start()
    cp_sink = [
        pltpu.make_async_copy(sink_ref.at[0, pl.ds(4 * g, 4)], sink_v.at[pl.ds(4 * g, 4)], sink_sem.at[g])
        for g in range(GROUPS)
    ]
    for cp in cp_sink:
        cp.start()

    barrier = pltpu.get_barrier_semaphore()

    @pl.loop(1, 32)
    def _(k):
        pl.semaphore_signal(
            barrier, inc=1,
            device_id=dev((x + k // 2) % 4, (y + k // 8) % 4, z, (core + k) % 2),
            device_id_type=MESH,
        )

    z_up = (z + 1) % 8
    z_dn = (z + 7) % 8
    for z_n in (z_up, z_dn):
        pl.semaphore_signal(barrier, inc=1, device_id=dev(x, y, z_n, core), device_id_type=MESH)

    cp_per.wait()
    pr = per_v[0].astype(F32)
    pi = per_v[1].astype(F32)
    prt = pr.T.astype(BF)
    pit = pi.T
    left[0:256, 0:256] = prt
    left[256:512, 256:512] = prt
    left[256:512, 0:256] = pit.astype(BF)
    left[0:256, 256:512] = (-pit).astype(BF)
    row = lax.broadcasted_iota(jnp.int32, (256, 256), 0) < 128
    col = lax.broadcasted_iota(jnp.int32, (256, 256), 1) < 128
    flip = jnp.where(row == col, 1.0, -1.0).astype(F32)
    br = (pr * flip).astype(BF)
    bi = -(pi * flip)
    bar[0:256, 0:256] = br
    bar[256:512, 256:512] = br
    bar[0:256, 256:512] = bi.astype(BF)
    bar[256:512, 0:256] = (-bi).astype(BF)

    cp_src.wait()
    pl.semaphore_wait(barrier, 33)

    me8 = x * 2 + core
    first = []
    for r in range(2):
        for far in range(2):
            xd = (2 * (y // 2) + r + y + 2 * far) % 4
            yd = (y + 2 * far) % 4
            for lh in range(2):
                src = src_v.at[:, :, pl.ds(16 * r, 16), pl.ds(128 * lh, 128)]
                dst = sring.at[0, me8]
                k = (r * 2 + far) * 2 + lh
                cp = pltpu.make_async_remote_copy(
                    src, dst, s1_send.at[k], s1_recv.at[me8],
                    device_id=dev(xd, yd, z, lh), device_id_type=MESH,
                )
                if far:
                    cp.start()
                    first.append((cp, None))
                else:
                    mine = jnp.logical_and(xd == x, core == lh)

                    @pl.when(jnp.logical_not(mine))
                    def _():
                        cp.start()

                    @pl.when(mine)
                    def _():
                        pltpu.make_async_copy(src, dst, s1_recv.at[me8]).start()

                    first.append((cp, jnp.logical_not(mine)))

    def ring(slot_from, slot_to, z_n, ch):
        return pltpu.make_async_remote_copy(
            sring.at[slot_from, pl.ds(4 * ch, 4)], sring.at[slot_to, pl.ds(4 * ch, 4)],
            ring_send.at[slot_from, ch] if z_n is z_up else ring_send.at[8 + slot_from, ch],
            ring_recv.at[slot_to, ch],
            device_id=dev(x, y, z_n, core), device_id_type=MESH,
        )

    ring_cps = []

    def ring_step(k, ch):
        up_from, dn_from = k - 1, (9 - k) % 8
        if k > 1:
            if k < 4 or ch == 0:
                ring_wait(up_from, ch)
            if k < 4 or ch == 1:
                ring_wait(dn_from, ch)
        if k < 4 or ch == 0:
            cp = ring(up_from, k, z_up, ch)
            cp.start()
            ring_cps.append(cp)
        if k < 4 or ch == 1:
            cp = ring(dn_from, 8 - k, z_dn, ch)
            cp.start()
            ring_cps.append(cp)

    waited = set()

    def ring_wait(slot, ch):
        if (slot, ch) in waited:
            return
        waited.add((slot, ch))
        ref = sring.at[slot, pl.ds(4 * ch, 4)]
        pltpu.make_async_copy(ref, ref, ring_recv.at[slot, ch]).wait()

    def place_source(d, ch):
        zs = (z + 8 - d) % 8
        h = zs // 4
        zl = zs % 4

        @pl.loop(0, 4)
        def _(s):
            for j in range(3):
                for c in range(2):
                    tile = sring[d, 4 * ch + s, j, c].astype(F32)
                    fs[h, zl, pl.ds(c * 24 + (4 * ch + s) * 3 + j, 16, STRIDE_S), :] = tile

    def turned(g):
        cp_sink[g].wait()

        @pl.loop(0, 4)
        def _(i4):
            i = 4 * g + i4
            prod = dot_t(left[:, 0:256], sink_v[i, 0]) + dot_t(left[:, 256:512], sink_v[i, 1])
            prod = prod.astype(BF)
            prod = jnp.concatenate([prod[0:256], prod[256:512]], axis=1)
            turn = jnp.dot(prod, bar[...], preferred_element_type=F32).astype(BF)
            for ys in range(4):
                for h in range(2):
                    for r in range(2):
                        b0 = ys * 64 + h * 32 + r * 16
                        for c in range(2):
                            for lh in range(2):
                                tout[ys, r, lh, g, c * 4 + i4, h] = turn[
                                    b0:b0 + 16, c * 256 + lh * 128:c * 256 + lh * 128 + 128
                                ]

    t_cps = []
    my_ys, my_r = block_of(x, y)

    def send_turned(g):
        for cls in range(7, -1, -1):
            if cls == 0:
                cp = pltpu.make_async_remote_copy(
                    tout.at[my_ys, my_r, 1 - core, g], recv.at[core, g],
                    t_send.at[g, 0], t_recv.at[core, g],
                    device_id=dev(x, y, z, 1 - core), device_id_type=MESH,
                )
                cp.start()
                t_cps.append(cp)
                pltpu.make_async_copy(tout.at[my_ys, my_r, core, g], recv.at[core, g], t_recv.at[core, g]).start()
                continue
            for lh in range(2):
                dx, dy = HOPS[cls][(g + lh) % 2]
                xd, yd = (x + dx) % 4, (y + dy) % 4
                ys, r = block_of(xd, yd)
                cp = pltpu.make_async_remote_copy(
                    tout.at[ys, r, lh, g], recv.at[2 * cls + core, g],
                    t_send.at[g, 2 * cls + lh], t_recv.at[2 * cls + core, g],
                    device_id=dev(xd, yd, z, lh), device_id_type=MESH,
                )
                cp.start()
                t_cps.append(cp)

    turned(0)
    send_turned(0)
    for k in range(8):
        ref = sring.at[0, k]
        pltpu.make_async_copy(ref, ref, s1_recv.at[k]).wait()
    ring_step(1, 0)
    ring_step(1, 1)
    turned(1)
    send_turned(1)
    place_source(0, 0)
    place_source(0, 1)
    turned(2)
    send_turned(2)
    for k in range(2, 5):
        for ch in range(2):
            ring_step(k, ch)
            if k < 4 or ch == 0:
                place_source(k - 1, ch)
            if k < 4 or ch == 1:
                place_source(9 - k, ch)
    for slot, ch in ((3, 1), (5, 0), (4, 0), (4, 1)):
        ring_wait(slot, ch)
        place_source(slot, ch)

    @pl.loop(0, 16)
    def _(b):
        for h in range(2):
            for c in range(2):
                rows = [fs[h, zl, pl.ds(b * STRIDE_S + c * 24, 24), :] for zl in range(4)]
                rows.append(jnp.zeros((32, 128), F32))
                sw[b, c * 128:c * 128 + 128, h * 128:h * 128 + 128] = jnp.concatenate(rows, axis=0).astype(BF)

    sign = jnp.where(lax.broadcasted_iota(jnp.int32, (16, 8, 128), 1) < 4, -1.0, 1.0).astype(F32)
    o_cps = []
    for g in range(GROUPS):
        for slot in range(16):
            ref = recv.at[slot, g]
            pltpu.make_async_copy(ref, ref, t_recv.at[slot, g]).wait()

        @pl.loop(0, 16)
        def _(slot):
            for ci in range(8):
                for h in range(2):
                    tile = recv[slot, g, ci, h].astype(F32)
                    ft[h, pl.ds(slot * 8 + ci, 16, STRIDE_T), :] = tile

        def step(b, acc):
            lhs = jnp.concatenate([ft[h, pl.ds(b * STRIDE_T, 128), :] for h in range(2)], axis=1).astype(BF)
            return acc + dot_t(lhs, sw[b])

        acc = lax.fori_loop(0, 16, step, jnp.zeros((128, 256), F32))
        a_re = acc[:, 0:128].reshape(16, 8, 128)
        a_im = acc[:, 128:256].reshape(16, 8, 128)
        oret[g] = a_re + sign * jnp.concatenate([a_im[:, 4:8], a_im[:, 0:4]], axis=1)

        for cls in range(8):
            if cls == 0:
                cp = pltpu.make_async_remote_copy(
                    oret.at[g, 1 - core], ogot.at[g, core], o_send.at[g, 0], o_recv.at[g, core],
                    device_id=dev(x, y, z, 1 - core), device_id_type=MESH,
                )
                cp.start()
                o_cps.append(cp)
                continue
            (dx0, dy0), (dx1, dy1) = HOPS[cls]
            odd = (g + core) % 2
            dx = dx0 + odd * (dx1 - dx0)
            dy = dy0 + odd * (dy1 - dy0)
            xd, yd = (x + 4 - dx) % 4, (y + 4 - dy) % 4
            for cs in range(2):
                cp = pltpu.make_async_remote_copy(
                    oret.at[g, 2 * cls + cs], ogot.at[g, 2 * cls + core],
                    o_send.at[g, 2 * cls + cs], o_recv.at[g, 2 * cls + core],
                    device_id=dev(xd, yd, z, cs), device_id_type=MESH,
                )
                cp.start()
                o_cps.append(cp)

    for g in range(GROUPS):
        for slot in range(2, 16):
            ref = ogot.at[g, slot]
            pltpu.make_async_copy(ref, ref, o_recv.at[g, slot]).wait()
        ref = ogot.at[g, 1 - core]
        pltpu.make_async_copy(ref, ref, o_recv.at[g, 1 - core]).wait()
        total = oret[g, core] + ogot[g, 1 - core]
        for slot in range(2, 16):
            total = total + ogot[g, slot]
        for c in range(2):
            out_ref[c, 4 * g:4 * g + 4, :] = total[4 * c:4 * c + 4, 0:96]

    for cp, cond in first:
        if cond is None:
            cp.wait_send()
        else:
            @pl.when(cond)
            def _():
                cp.wait_send()
    for cp in ring_cps + t_cps + o_cps:
        cp.wait_send()


def local(peram, sink_elementals, source_elementals, irrep):
    group_ops = sink_elementals.shape[1]
    dma = pltpu.SemaphoreType.DMA
    full = pl.pallas_call(
        kernel,
        out_shape=jax.ShapeDtypeStruct((2, 12, 96), F32),
        in_specs=[pl.BlockSpec(memory_space=pl.ANY)] * 3,
        out_specs=pl.BlockSpec(memory_space=pltpu.VMEM),
        scratch_shapes=[
            pltpu.VMEM((2, 256, 256), BF),
            pltpu.VMEM((12, 2, 256, 256), BF),
            pltpu.VMEM((3, 2, 32, 256), BF),
            pltpu.VMEM((512, 512), BF),
            pltpu.VMEM((512, 512), BF),
            pltpu.VMEM((4, 2, 2, 3, 8, 2, 16, 128), BF),
            pltpu.VMEM((16, 3, 8, 2, 16, 128), BF),
            pltpu.VMEM((8, 8, 3, 2, 16, 128), BF),
            pltpu.VMEM((2, 4, 16 * STRIDE_S, 128), F32),
            pltpu.VMEM((2, 16 * STRIDE_T, 128), F32),
            pltpu.VMEM((16, 256, 256), BF),
            pltpu.VMEM((3, 16, 8, 128), F32),
            pltpu.VMEM((3, 16, 8, 128), F32),
            dma((2,)),
            dma((3,)),
            dma((8,)),
            dma((8,)),
            dma((16, 2)),
            dma((8, 2)),
            dma((3, 16)),
            dma((16, 3)),
            dma((3, 16)),
            dma((3, 16)),
        ],
        compiler_params=pltpu.CompilerParams(
            collective_id=0, has_side_effects=True, vmem_limit_bytes=48 * 1024 * 1024
        ),
        cost_estimate=pl.CostEstimate(flops=7_000_000_000, bytes_accessed=4_000_000, transcendentals=0),
    )(peram, sink_elementals, source_elementals)
    first = lax.axis_index("op") * group_ops
    own_labels = lax.dynamic_slice_in_dim(irrep, first, group_ops, 0)
    same = (own_labels[:, None] == irrep[None, :]).astype(F32)
    return (full * same[None, :, :])[None]


def solution(mesh):
    return jax.shard_map(
        local,
        mesh=mesh,
        in_specs=(
            P("tm", None, None, None),
            P("tm", "op", None, None, None),
            P("tm", None, "op", None),
            P(),
        ),
        out_specs=P("tm", None, "op", None),
        check_vma=False,
    )
```

```python
import jax
import jax.numpy as jnp
from jax import lax
from jax.experimental import pallas as pl
from jax.experimental.pallas import tpu as pltpu
from jax.sharding import PartitionSpec as P

MESH = pl.DeviceIdType.MESH
BF = jnp.bfloat16
F32 = jnp.float32
GROUPS = 3
STRIDE_T = 136
STRIDE_S = 48

HOPS = (
    ((0, 0), (0, 0)),
    ((1, 0), (1, 0)),
    ((3, 0), (3, 0)),
    ((0, 1), (0, 1)),
    ((0, 3), (0, 3)),
    ((3, 3), (1, 1)),
    ((1, 3), (3, 1)),
    ((2, 0), (0, 2)),
)


def dot_t(a, b):
    return lax.dot_general(a, b, (((1,), (1,)), ((), ())), preferred_element_type=F32)


def kernel(
    peram_ref, sink_ref, src_ref, lab_ref, out_ref,
    per_v, sink_v, src_v, lab_v, left, bar, tout, recv, sring, fs, ft, lhs, sw, oret, ogot,
    in_sem, sink_sem, s1_send, s1_recv, ring_send, ring_recv, t_send, t_recv, o_send, o_recv, answer,
):
    tm = lax.axis_index("tm")
    op = lax.axis_index("op")
    core = tm % 2
    x = (tm // 2) % 4
    y = op // 2
    z = (op % 2) * 4 + tm // 8

    def dev(x_, y_, z_, c_):
        return ((z_ % 4) * 8 + x_ * 2 + c_, y_ * 2 + z_ // 4)

    def block_of(x_, y_):
        p = (x_ + 4 - y_) % 4
        return y_ % 2 + 2 * (p // 2), p % 2

    cp_src = pltpu.make_async_copy(src_ref, src_v, in_sem.at[0])
    cp_per = pltpu.make_async_copy(peram_ref.at[0], per_v, in_sem.at[1])
    cp_lab = pltpu.make_async_copy(lab_ref, lab_v, in_sem.at[2])
    cp_src.start()
    cp_per.start()
    cp_lab.start()
    cp_sink = [
        pltpu.make_async_copy(sink_ref.at[0, pl.ds(4 * g, 4)], sink_v.at[pl.ds(4 * g, 4)], sink_sem.at[g])
        for g in range(GROUPS)
    ]
    for cp in cp_sink:
        cp.start()

    barrier = pltpu.get_barrier_semaphore()

    @pl.loop(1, 32)
    def _(k):
        pl.semaphore_signal(
            barrier, inc=1,
            device_id=dev((x + k // 2) % 4, (y + k // 8) % 4, z, (core + k) % 2),
            device_id_type=MESH,
        )

    z_up = (z + 1) % 8
    z_dn = (z + 7) % 8
    later_up = z < 7
    later_dn = z == 0
    for z_n, later in ((z_up, later_up), (z_dn, later_dn)):
        @pl.when(later)
        def _():
            pl.semaphore_signal(barrier, inc=1, device_id=dev(x, y, z_n, core), device_id_type=MESH)

    def turned(g):
        cp_sink[g].wait()
        prods = []
        for i4 in range(4):
            i = 4 * g + i4
            elem = jnp.concatenate([sink_v[i, 0], sink_v[i, 1]], axis=1)
            prod = dot_t(left[...], elem).astype(BF)
            prods.append(jnp.concatenate([prod[0:256], prod[256:512]], axis=1))
        for i4 in range(4):
            turn = jnp.dot(prods[i4], bar[...], preferred_element_type=F32).astype(BF)
            for ys in range(4):
                for h in range(2):
                    for r in range(2):
                        b0 = ys * 64 + h * 32 + r * 16
                        for c in range(2):
                            for lh in range(2):
                                tout[ys, r, lh, g, c * 4 + i4, h] = turn[
                                    b0:b0 + 16, c * 256 + lh * 128:c * 256 + lh * 128 + 128
                                ]

    cp_src.wait()
    pl.semaphore_wait(barrier, 31 + jnp.where(z > 0, 1, 0) + jnp.where(z == 7, 1, 0))
    for z_n, later, at in ((z_up, later_up, 1), (z_dn, later_dn, 0)):
        @pl.when(jnp.logical_not(later))
        def _():
            pl.semaphore_signal(answer.at[at], inc=1, device_id=dev(x, y, z_n, core), device_id_type=MESH)

    first = []
    for r in range(2):
        for far in range(2):
            xd = (2 * (y // 2) + r + y + 2 * far) % 4
            yd = (y + 2 * far) % 4
            for lh in range(2):
                src = src_v.at[:, :, pl.ds(16 * r, 16), pl.ds(128 * lh, 128)]
                me8 = ((x + 4 - xd) % 4) * 2 + core
                dst = sring.at[0, me8]
                k = (r * 2 + far) * 2 + lh
                cp = pltpu.make_async_remote_copy(
                    src, dst, s1_send.at[k], s1_recv.at[me8],
                    device_id=dev(xd, yd, z, lh), device_id_type=MESH,
                )
                if far:
                    cp.start()
                    first.append((cp, None))
                else:
                    mine = jnp.logical_and(xd == x, core == lh)

                    @pl.when(jnp.logical_not(mine))
                    def _():
                        cp.start()

                    @pl.when(mine)
                    def _():
                        pltpu.make_async_copy(src, dst, s1_recv.at[me8]).start()

                    first.append((cp, jnp.logical_not(mine)))

    def ring(slot_from, slot_to, z_n, ch):
        return pltpu.make_async_remote_copy(
            sring.at[slot_from, pl.ds(2 * ch, 2)], sring.at[slot_to, pl.ds(2 * ch, 2)],
            ring_send.at[slot_from, ch] if z_n is z_up else ring_send.at[8 + slot_from, ch],
            ring_recv.at[slot_to, ch],
            device_id=dev(x, y, z_n, core), device_id_type=MESH,
        )

    ring_cps = []

    def ring_step(k, ch):
        up_from, dn_from = k - 1, (9 - k) % 8
        if k < 4:
            ring_wait(up_from, ch)
            cp = ring(up_from, k, z_up, ch)
            cp.start()
            ring_cps.append(cp)
        ring_wait(dn_from, ch)
        cp = ring(dn_from, 8 - k, z_dn, ch)
        cp.start()
        ring_cps.append(cp)

    waited = set()

    def ring_wait(slot, ch):
        if (slot, ch) in waited:
            return
        waited.add((slot, ch))
        if slot == 0:
            for k in (2 * ch, 2 * ch + 1):
                ref = sring.at[0, k]
                pltpu.make_async_copy(ref, ref, s1_recv.at[k]).wait()
            return
        ref = sring.at[slot, pl.ds(2 * ch, 2)]
        pltpu.make_async_copy(ref, ref, ring_recv.at[slot, ch]).wait()

    def place_source(d):
        zs = (z + 8 - d) % 8
        h = zs // 4
        zl = zs % 4

        @pl.loop(0, 4)
        def _(ch):
            xs = (x + ch) % 4
            for cs in range(2):
                for j in range(3):
                    for c in range(2):
                        tile = sring[d, 2 * ch + cs, j, c].astype(F32)
                        fs[h, zl, pl.ds(xs * 6 + c * 24 + cs * 3 + j, 16, STRIDE_S), :] = tile

        for b in range(16):
            sw[h, b, zl] = fs[h, zl, pl.ds(b * STRIDE_S, 48), :].astype(BF)

    t_cps = []
    my_ys, my_r = block_of(x, y)

    def send_turned(g):
        for cls in range(7, -1, -1):
            if cls == 0:
                cp = pltpu.make_async_remote_copy(
                    tout.at[my_ys, my_r, 1 - core, g], recv.at[core, g],
                    t_send.at[g, 0], t_recv.at[core, g],
                    device_id=dev(x, y, z, 1 - core), device_id_type=MESH,
                )
                cp.start()
                t_cps.append(cp)
                pltpu.make_async_copy(tout.at[my_ys, my_r, core, g], recv.at[core, g], t_recv.at[core, g]).start()
                continue
            for lh in range(2):
                dx, dy = HOPS[cls][(g + lh) % 2]
                xd, yd = (x + dx) % 4, (y + dy) % 4
                ys, r = block_of(xd, yd)
                cp = pltpu.make_async_remote_copy(
                    tout.at[ys, r, lh, g], recv.at[2 * cls + core, g],
                    t_send.at[g, 2 * cls + lh], t_recv.at[2 * cls + core, g],
                    device_id=dev(xd, yd, z, lh), device_id_type=MESH,
                )
                cp.start()
                t_cps.append(cp)

    def gather_rows(g):
        @pl.loop(0, 8)
        def _(k):
            cls = (8 - k) % 8
            for cs in range(2):
                ref = recv.at[2 * cls + cs, g]
                pltpu.make_async_copy(ref, ref, t_recv.at[2 * cls + cs, g]).wait()
                for ci in range(8):
                    for h in range(2):
                        tile = recv[2 * cls + cs, g, ci, h].astype(F32)
                        ft[h, pl.ds(cls * 16 + cs * 8 + ci, 16, STRIDE_T), :] = tile
            for b in range(16):
                for h in range(2):
                    tile = ft[h, pl.ds(b * STRIDE_T + cls * 16, 16), :]
                    lhs[b, pl.ds(g * 128 + cls * 16, 16), h * 128:h * 128 + 128] = tile.astype(BF)

    cp_per.wait()
    pr = per_v[0].astype(F32)
    pi = per_v[1].astype(F32)
    prt = pr.T.astype(BF)
    pit = pi.T
    left[0:256, 0:256] = prt
    left[256:512, 256:512] = prt
    left[256:512, 0:256] = pit.astype(BF)
    left[0:256, 256:512] = (-pit).astype(BF)
    row = lax.broadcasted_iota(jnp.int32, (256, 256), 0) < 128
    col = lax.broadcasted_iota(jnp.int32, (256, 256), 1) < 128
    flip = jnp.where(row == col, 1.0, -1.0).astype(F32)
    br = (pr * flip).astype(BF)
    bi = -(pi * flip)
    bar[0:256, 0:256] = br
    bar[256:512, 256:512] = br
    bar[0:256, 256:512] = bi.astype(BF)
    bar[256:512, 0:256] = (-bi).astype(BF)

    turned(0)
    for later, at in ((later_up, 0), (later_dn, 1)):
        @pl.when(later)
        def _():
            pl.semaphore_wait(answer.at[at], 1)
    ring_step(1, 0)
    send_turned(0)
    for ch in range(1, 4):
        ring_step(1, ch)
    turned(1)
    send_turned(1)
    place_source(0)
    ring_step(2, 0)
    ring_step(2, 1)
    turned(2)
    send_turned(2)
    ring_step(2, 2)
    ring_step(2, 3)
    place_source(1)
    place_source(7)
    for ch in range(4):
        ring_step(3, ch)
    place_source(2)
    place_source(6)
    gather_rows(0)
    for ch in range(4):
        ring_step(4, ch)
    gather_rows(1)
    for slot in (5, 3, 4):
        for ch in range(4):
            ring_wait(slot, ch)
        place_source(slot)

    cp_lab.wait()
    labels = jnp.broadcast_to(lab_v[...].astype(F32), (8, 96))
    lane = lax.broadcasted_iota(jnp.int32, (8, 96), 1)
    sub = lax.broadcasted_iota(jnp.int32, (8, 96), 0) % 4
    same = []
    for g in range(GROUPS):
        own = jnp.sum(jnp.where(lane == op * 12 + 4 * g + sub, labels, 0.0), axis=1, keepdims=True)
        same.append((own == labels).astype(F32))

    o_cps = []

    def contract(g0, n):
        rows = n * 128
        acc = None
        for b in range(16):
            right = jnp.concatenate([sw[0, b].reshape(192, 128), sw[1, b].reshape(192, 128)], axis=1)
            part = dot_t(lhs[b, g0 * 128:g0 * 128 + rows, :], right)
            acc = part if acc is None else acc + part
        acc = jnp.concatenate([acc, jnp.zeros((rows, 64), F32)], axis=1)
        other = pltpu.roll(acc, 232, 1).reshape(n * 16, 8, 256)
        sign = jnp.where(lax.broadcasted_iota(jnp.int32, (n * 16, 8, 256), 1) < 4, -1.0, 1.0).astype(F32)
        other = jnp.concatenate([other[:, 4:8], other[:, 0:4]], axis=1)
        oret[g0:g0 + n] = (acc.reshape(n * 16, 8, 256) + sign * other).reshape(n, 16, 8, 256)

    def give_back(gs, cls):
        g = gs[0]
        part = pl.ds(g, len(gs))
        if cls == 0:
            cp = pltpu.make_async_remote_copy(
                oret.at[part, 1 - core], ogot.at[part, core], o_send.at[g, 0], o_recv.at[g, core],
                device_id=dev(x, y, z, 1 - core), device_id_type=MESH,
            )
            cp.start()
            o_cps.append(cp)
            return
        (dx0, dy0), (dx1, dy1) = HOPS[cls]
        odd = (g + core) % 2
        dx = dx0 + odd * (dx1 - dx0)
        dy = dy0 + odd * (dy1 - dy0)
        xd, yd = (x + 4 - dx) % 4, (y + 4 - dy) % 4
        for cs in range(2):
            cp = pltpu.make_async_remote_copy(
                oret.at[part, 2 * cls + cs], ogot.at[part, 2 * cls + core],
                o_send.at[g, 2 * cls + cs], o_recv.at[g, 2 * cls + core],
                device_id=dev(xd, yd, z, cs), device_id_type=MESH,
            )
            cp.start()
            o_cps.append(cp)

    def got_back(gs, slot):
        ref = ogot.at[pl.ds(gs[0], len(gs)), slot]
        pltpu.make_async_copy(ref, ref, o_recv.at[gs[0], slot]).wait()

    def total(g):
        out = oret[g, core] + ogot[g, 1 - core]
        for slot in range(2, 16):
            out = out + ogot[g, slot]
        out = jnp.concatenate([out[:, 48 * k:48 * k + 24] for k in range(4)], axis=1) * same[g]
        for c in range(2):
            for i4 in range(4):
                out_ref[4 * g + i4, c:c + 1, :] = out[4 * c + i4:4 * c + i4 + 1, :]

    def pairs(cls):
        return ((0, 1),) if cls < 5 else ((0,), (1,))

    contract(0, 2)
    for cls in range(7, -1, -1):
        for gs in pairs(cls):
            give_back(gs, cls)
    gather_rows(2)
    contract(2, 1)
    for cls in range(7, -1, -1):
        give_back((2,), cls)
    for cls in range(1, 8):
        for gs in pairs(cls):
            for cs in range(2):
                got_back(gs, 2 * cls + cs)
    got_back((0, 1), 1 - core)
    total(0)
    total(1)
    for slot in range(2, 16):
        got_back((2,), slot)
    got_back((2,), 1 - core)
    total(2)

    for cp, cond in first:
        if cond is None:
            cp.wait_send()
        else:
            @pl.when(cond)
            def _():
                cp.wait_send()
    for cp in ring_cps + t_cps + o_cps:
        cp.wait_send()


def local(peram, sink_elementals, source_elementals, irrep):
    dma = pltpu.SemaphoreType.DMA
    full = pl.pallas_call(
        kernel,
        out_shape=jax.ShapeDtypeStruct((12, 2, 96), F32),
        in_specs=[pl.BlockSpec(memory_space=pl.ANY)] * 4,
        out_specs=pl.BlockSpec(memory_space=pltpu.VMEM),
        scratch_shapes=[
            pltpu.VMEM((2, 256, 256), BF),
            pltpu.VMEM((12, 2, 256, 256), BF),
            pltpu.VMEM((3, 2, 32, 256), BF),
            pltpu.VMEM((1, 96), jnp.int32),
            pltpu.VMEM((512, 512), BF),
            pltpu.VMEM((512, 512), BF),
            pltpu.VMEM((4, 2, 2, 3, 8, 2, 16, 128), BF),
            pltpu.VMEM((16, 3, 8, 2, 16, 128), BF),
            pltpu.VMEM((8, 8, 3, 2, 16, 128), BF),
            pltpu.VMEM((2, 4, 16 * STRIDE_S, 128), F32),
            pltpu.VMEM((2, 16 * STRIDE_T, 128), F32),
            pltpu.VMEM((16, 384, 256), BF),
            pltpu.VMEM((2, 16, 4, 48, 128), BF),
            pltpu.VMEM((3, 16, 8, 256), F32),
            pltpu.VMEM((3, 16, 8, 256), F32),
            dma((3,)),
            dma((3,)),
            dma((8,)),
            dma((8,)),
            dma((16, 4)),
            dma((8, 4)),
            dma((3, 16)),
            dma((16, 3)),
            dma((3, 16)),
            dma((3, 16)),
            pltpu.SemaphoreType.REGULAR((2,)),
        ],
        compiler_params=pltpu.CompilerParams(
            collective_id=0, has_side_effects=True, vmem_limit_bytes=60 * 1024 * 1024
        ),
        cost_estimate=pl.CostEstimate(flops=7_000_000_000, bytes_accessed=4_000_000, transcendentals=0),
    )(peram, sink_elementals, source_elementals, irrep.reshape(1, 96))
    return jnp.swapaxes(full, 0, 1)[None]


def solution(mesh):
    return jax.shard_map(
        local,
        mesh=mesh,
        in_specs=(
            P("tm", None, None, None),
            P("tm", "op", None, None, None),
            P("tm", None, "op", None),
            P(),
        ),
        out_specs=P("tm", None, "op", None),
        check_vma=False,
    )
```

```python
import jax
import jax.numpy as jnp
from jax import lax
from jax.experimental import pallas as pl
from jax.experimental.pallas import tpu as pltpu
from jax.sharding import PartitionSpec as P

MESH = pl.DeviceIdType.MESH
BF = jnp.bfloat16
F32 = jnp.float32
GROUPS = 3
STRIDE_T = 136
STRIDE_S = 48

HOPS = (
    ((0, 0), (0, 0)),
    ((1, 0), (1, 0)),
    ((3, 0), (3, 0)),
    ((0, 1), (0, 1)),
    ((0, 3), (0, 3)),
    ((3, 3), (1, 1)),
    ((1, 3), (3, 1)),
    ((2, 0), (0, 2)),
)


def dot_t(a, b):
    return lax.dot_general(a, b, (((1,), (1,)), ((), ())), preferred_element_type=F32)


def kernel(
    peram_ref, sink_ref, src_ref, lab_ref, out_ref,
    per_v, sink_v, src_v, lab_v, left, bar, tout, recv, sring, fs, ft, lhs, sw, oret, ogot,
    in_sem, sink_sem, s1_send, s1_recv, ring_send, ring_recv, t_send, t_recv, o_send, o_recv, answer,
):
    tm = lax.axis_index("tm")
    op = lax.axis_index("op")
    core = tm % 2
    x = (tm // 2) % 4
    y = op // 2
    z = (op % 2) * 4 + tm // 8

    def dev(x_, y_, z_, c_):
        return ((z_ % 4) * 8 + x_ * 2 + c_, y_ * 2 + z_ // 4)

    def block_of(x_, y_):
        p = (x_ + 4 - y_) % 4
        return y_ % 2 + 2 * (p // 2), p % 2

    cp_src = pltpu.make_async_copy(src_ref, src_v, in_sem.at[0])
    cp_per = pltpu.make_async_copy(peram_ref.at[0], per_v, in_sem.at[1])
    cp_lab = pltpu.make_async_copy(lab_ref, lab_v, in_sem.at[2])
    cp_src.start()
    cp_per.start()
    cp_lab.start()
    cp_sink = [
        pltpu.make_async_copy(sink_ref.at[0, pl.ds(4 * g, 4)], sink_v.at[pl.ds(4 * g, 4)], sink_sem.at[g])
        for g in range(GROUPS)
    ]
    for cp in cp_sink:
        cp.start()

    barrier = pltpu.get_barrier_semaphore()

    @pl.loop(1, 32)
    def _(k):
        pl.semaphore_signal(
            barrier, inc=1,
            device_id=dev((x + k // 2) % 4, (y + k // 8) % 4, z, (core + k) % 2),
            device_id_type=MESH,
        )

    z_up = (z + 1) % 8
    z_dn = (z + 7) % 8
    later_up = z < 7
    later_dn = z == 0
    for z_n, later in ((z_up, later_up), (z_dn, later_dn)):
        @pl.when(later)
        def _():
            pl.semaphore_signal(barrier, inc=1, device_id=dev(x, y, z_n, core), device_id_type=MESH)

    def turned(g):
        cp_sink[g].wait()
        prods = []
        for i4 in range(4):
            i = 4 * g + i4
            elem = jnp.concatenate([sink_v[i, 0], sink_v[i, 1]], axis=1)
            prod = dot_t(left[...], elem).astype(BF)
            prods.append(jnp.concatenate([prod[0:256], prod[256:512]], axis=1))
        for i4 in range(4):
            turn = jnp.dot(prods[i4], bar[...], preferred_element_type=F32).astype(BF)
            for ys in range(4):
                for h in range(2):
                    for r in range(2):
                        b0 = ys * 64 + h * 32 + r * 16
                        for c in range(2):
                            for lh in range(2):
                                tout[ys, r, lh, g, c * 4 + i4, h] = turn[
                                    b0:b0 + 16, c * 256 + lh * 128:c * 256 + lh * 128 + 128
                                ]

    cp_src.wait()
    pl.semaphore_wait(barrier, 31 + jnp.where(z > 0, 1, 0) + jnp.where(z == 7, 1, 0))
    for z_n, later, at in ((z_up, later_up, 1), (z_dn, later_dn, 0)):
        @pl.when(jnp.logical_not(later))
        def _():
            pl.semaphore_signal(answer.at[at], inc=1, device_id=dev(x, y, z_n, core), device_id_type=MESH)

    first = []
    for r in range(2):
        for far in range(2):
            xd = (2 * (y // 2) + r + y + 2 * far) % 4
            yd = (y + 2 * far) % 4
            for lh in range(2):
                src = src_v.at[:, :, pl.ds(16 * r, 16), pl.ds(128 * lh, 128)]
                me8 = ((x + 4 - xd) % 4) * 2 + core
                dst = sring.at[0, me8]
                k = (r * 2 + far) * 2 + lh
                cp = pltpu.make_async_remote_copy(
                    src, dst, s1_send.at[k], s1_recv.at[me8],
                    device_id=dev(xd, yd, z, lh), device_id_type=MESH,
                )
                if far:
                    cp.start()
                    first.append((cp, None))
                else:
                    mine = jnp.logical_and(xd == x, core == lh)

                    @pl.when(jnp.logical_not(mine))
                    def _():
                        cp.start()

                    @pl.when(mine)
                    def _():
                        pltpu.make_async_copy(src, dst, s1_recv.at[me8]).start()

                    first.append((cp, jnp.logical_not(mine)))

    def ring(slot_from, slot_to, z_n, ch):
        return pltpu.make_async_remote_copy(
            sring.at[slot_from, pl.ds(2 * ch, 2)], sring.at[slot_to, pl.ds(2 * ch, 2)],
            ring_send.at[slot_from, ch] if z_n is z_up else ring_send.at[8 + slot_from, ch],
            ring_recv.at[slot_to, ch],
            device_id=dev(x, y, z_n, core), device_id_type=MESH,
        )

    ring_cps = []

    def ring_up(k, ch):
        ring_wait(k - 1, ch)
        cp = ring(k - 1, k, z_up, ch)
        cp.start()
        ring_cps.append(cp)

    def ring_down(k, ch, cond=None):
        ring_wait((9 - k) % 8, ch)
        cp = ring((9 - k) % 8, 8 - k, z_dn, ch)
        if cond is None:
            cp.start()
        else:
            pl.when(cond)(cp.start)
        return cp

    def ring_step(k, ch):
        ring_cps.append(ring_down(k, ch))
        if k < 4:
            ring_up(k, ch)

    waited = set()

    def ring_wait(slot, ch):
        if (slot, ch) in waited:
            return
        waited.add((slot, ch))
        if slot == 0:
            for k in (2 * ch, 2 * ch + 1):
                ref = sring.at[0, k]
                pltpu.make_async_copy(ref, ref, s1_recv.at[k]).wait()
            return
        ref = sring.at[slot, pl.ds(2 * ch, 2)]
        pltpu.make_async_copy(ref, ref, ring_recv.at[slot, ch]).wait()

    def place_source(d):
        zs = (z + 8 - d) % 8
        h = zs // 4
        zl = zs % 4

        @pl.loop(0, 4)
        def _(ch):
            xs = (x + ch) % 4
            for cs in range(2):
                for j in range(3):
                    for c in range(2):
                        tile = sring[d, 2 * ch + cs, j, c].astype(F32)
                        fs[h, zl, pl.ds(xs * 6 + c * 24 + cs * 3 + j, 16, STRIDE_S), :] = tile

    t_cps = []
    my_ys, my_r = block_of(x, y)

    def send_turned(g):
        for cls in (0, 1, 2, 3, 4, 7, 5, 6):
            if cls == 0:
                cp = pltpu.make_async_remote_copy(
                    tout.at[my_ys, my_r, 1 - core, g], recv.at[core, g],
                    t_send.at[g, 0], t_recv.at[core, g],
                    device_id=dev(x, y, z, 1 - core), device_id_type=MESH,
                )
                cp.start()
                t_cps.append(cp)
                pltpu.make_async_copy(tout.at[my_ys, my_r, core, g], recv.at[core, g], t_recv.at[core, g]).start()
                continue
            for lh in range(2):
                dx, dy = HOPS[cls][lh]
                xd, yd = (x + dx) % 4, (y + dy) % 4
                ys, r = block_of(xd, yd)
                cp = pltpu.make_async_remote_copy(
                    tout.at[ys, r, lh, g], recv.at[2 * cls + core, g],
                    t_send.at[g, 2 * cls + lh], t_recv.at[2 * cls + core, g],
                    device_id=dev(xd, yd, z, lh), device_id_type=MESH,
                )
                cp.start()
                t_cps.append(cp)

    def gather_rows(g):
        @pl.loop(0, 8)
        def _(k):
            cls = k
            for cs in range(2):
                ref = recv.at[2 * cls + cs, g]
                pltpu.make_async_copy(ref, ref, t_recv.at[2 * cls + cs, g]).wait()
                for ci in range(8):
                    for h in range(2):
                        tile = recv[2 * cls + cs, g, ci, h].astype(F32)
                        ft[h, pl.ds(cls * 16 + cs * 8 + ci, 16, STRIDE_T), :] = tile
            for b in range(16):
                for h in range(2):
                    tile = ft[h, pl.ds(b * STRIDE_T + cls * 16, 16), :]
                    lhs[b, pl.ds(g * 128 + cls * 16, 16), h * 128:h * 128 + 128] = tile.astype(BF)

    cp_per.wait()
    pr = per_v[0].astype(F32)
    pi = per_v[1].astype(F32)
    prt = pr.T.astype(BF)
    pit = pi.T
    left[0:256, 0:256] = prt
    left[256:512, 256:512] = prt
    left[256:512, 0:256] = pit.astype(BF)
    left[0:256, 256:512] = (-pit).astype(BF)
    row = lax.broadcasted_iota(jnp.int32, (256, 256), 0) < 128
    col = lax.broadcasted_iota(jnp.int32, (256, 256), 1) < 128
    flip = jnp.where(row == col, 1.0, -1.0).astype(F32)
    br = (pr * flip).astype(BF)
    bi = -(pi * flip)
    bar[0:256, 0:256] = br
    bar[256:512, 256:512] = br
    bar[0:256, 256:512] = bi.astype(BF)
    bar[256:512, 0:256] = (-bi).astype(BF)

    turned(0)
    send_turned(0)
    turned(1)

    @pl.when(later_up)
    def _():
        pl.semaphore_wait(answer.at[0], 1)

    for ch in range(4):
        ring_up(1, ch)
        ring_cps.append(ring_down(1, ch, jnp.logical_not(later_dn)))
        if ch == 1:
            send_turned(1)
    turned(2)
    send_turned(2)

    @pl.when(later_dn)
    def _():
        pl.semaphore_wait(answer.at[1], 1)
        for ch in range(4):
            ring(0, 7, z_dn, ch).start()

    place_source(0)
    ring_step(2, 0)
    ring_step(2, 1)
    ring_step(2, 2)
    ring_step(2, 3)
    place_source(1)
    place_source(7)
    for ch in range(4):
        ring_step(3, ch)
    place_source(2)
    place_source(6)
    gather_rows(0)
    for ch in range(4):
        ring_step(4, ch)
    gather_rows(1)
    for slot in (5, 3, 4):
        if slot == 4:
            gather_rows(2)
        for ch in range(4):
            ring_wait(slot, ch)
        place_source(slot)

    cp_lab.wait()
    labels = jnp.broadcast_to(lab_v[...].astype(F32), (8, 96))
    lane = lax.broadcasted_iota(jnp.int32, (8, 96), 1)
    sub = lax.broadcasted_iota(jnp.int32, (8, 96), 0) % 4
    same = []
    for g in range(GROUPS):
        own = jnp.sum(jnp.where(lane == op * 12 + 4 * g + sub, labels, 0.0), axis=1, keepdims=True)
        same.append((own == labels).astype(F32))

    o_cps = []

    @pl.loop(0, 16, unroll=2)
    def _(b):
        for h in range(2):
            for c in range(2):
                rows = [fs[h, zl, pl.ds(b * STRIDE_S + c * 24, 24), :] for zl in range(4)]
                if c == 0:
                    rows.append(jnp.zeros((32, 128), F32))
                rows = jnp.concatenate(rows, axis=0).astype(BF)
                sw[b, c * 128:c * 128 + rows.shape[0], h * 128:h * 128 + 128] = rows

    acc = dot_t(lhs[0], sw[0])
    for b in range(1, 16):
        acc = acc + dot_t(lhs[b], sw[b])
    with_re = acc[:, 0:128].reshape(48, 8, 128)
    with_im = jnp.concatenate([acc[:, 128:224], jnp.zeros((384, 32), F32)], axis=1).reshape(48, 8, 128)
    with_im = jnp.concatenate([with_im[:, 4:8], with_im[:, 0:4]], axis=1)
    sign = jnp.where(lax.broadcasted_iota(jnp.int32, (48, 8, 128), 1) < 4, -1.0, 1.0).astype(F32)
    oret[...] = (with_re + sign * with_im).reshape(3, 16, 8, 128)

    for cls in (7, 6, 5, 4, 3, 2, 1, 0):
        if cls == 0:
            cp = pltpu.make_async_remote_copy(
                oret.at[:, 1 - core], ogot.at[:, core], o_send.at[0], o_recv.at[core],
                device_id=dev(x, y, z, 1 - core), device_id_type=MESH,
            )
            cp.start()
            o_cps.append(cp)
            continue
        (dx0, dy0), (dx1, dy1) = HOPS[cls]
        dx = dx0 + core * (dx1 - dx0)
        dy = dy0 + core * (dy1 - dy0)
        xd, yd = (x + 4 - dx) % 4, (y + 4 - dy) % 4
        for cs in range(2):
            cp = pltpu.make_async_remote_copy(
                oret.at[:, 2 * cls + cs], ogot.at[:, 2 * cls + core],
                o_send.at[2 * cls + cs], o_recv.at[2 * cls + core],
                device_id=dev(xd, yd, z, cs), device_id_type=MESH,
            )
            cp.start()
            o_cps.append(cp)

    total = oret[:, core]
    ref = ogot.at[:, 1 - core]
    pltpu.make_async_copy(ref, ref, o_recv.at[1 - core]).wait()
    total = total + ogot[:, 1 - core]
    for slot in range(2, 16):
        ref = ogot.at[:, slot]
        pltpu.make_async_copy(ref, ref, o_recv.at[slot]).wait()
        total = total + ogot[:, slot]
    for g in range(GROUPS):
        out = total[g, :, 0:96] * same[g]
        for c in range(2):
            for i4 in range(4):
                out_ref[4 * g + i4, c:c + 1, :] = out[4 * c + i4:4 * c + i4 + 1, :]

    for cp, cond in first:
        if cond is None:
            cp.wait_send()
        else:
            @pl.when(cond)
            def _():
                cp.wait_send()
    for cp in ring_cps + t_cps + o_cps:
        cp.wait_send()


def local(peram, sink_elementals, source_elementals, irrep):
    dma = pltpu.SemaphoreType.DMA
    full = pl.pallas_call(
        kernel,
        out_shape=jax.ShapeDtypeStruct((12, 2, 96), F32),
        in_specs=[pl.BlockSpec(memory_space=pl.ANY)] * 4,
        out_specs=pl.BlockSpec(memory_space=pltpu.VMEM),
        scratch_shapes=[
            pltpu.VMEM((2, 256, 256), BF),
            pltpu.VMEM((12, 2, 256, 256), BF),
            pltpu.VMEM((3, 2, 32, 256), BF),
            pltpu.VMEM((1, 96), jnp.int32),
            pltpu.VMEM((512, 512), BF),
            pltpu.VMEM((512, 512), BF),
            pltpu.VMEM((4, 2, 2, 3, 8, 2, 16, 128), BF),
            pltpu.VMEM((16, 3, 8, 2, 16, 128), BF),
            pltpu.VMEM((8, 8, 3, 2, 16, 128), BF),
            pltpu.VMEM((2, 4, 16 * STRIDE_S, 128), F32),
            pltpu.VMEM((2, 16 * STRIDE_T, 128), F32),
            pltpu.VMEM((16, 384, 256), BF),
            pltpu.VMEM((16, 224, 256), BF),
            pltpu.VMEM((3, 16, 8, 128), F32),
            pltpu.VMEM((3, 16, 8, 128), F32),
            dma((3,)),
            dma((3,)),
            dma((8,)),
            dma((8,)),
            dma((16, 4)),
            dma((8, 4)),
            dma((3, 16)),
            dma((16, 3)),
            dma((16,)),
            dma((16,)),
            pltpu.SemaphoreType.REGULAR((2,)),
        ],
        compiler_params=pltpu.CompilerParams(
            collective_id=0, has_side_effects=True, vmem_limit_bytes=60 * 1024 * 1024
        ),
        cost_estimate=pl.CostEstimate(flops=7_000_000_000, bytes_accessed=4_000_000, transcendentals=0),
    )(peram, sink_elementals, source_elementals, irrep.reshape(1, 96))
    return jnp.swapaxes(full, 0, 1)[None]


def solution(mesh):
    return jax.shard_map(
        local,
        mesh=mesh,
        in_specs=(
            P("tm", None, None, None),
            P("tm", "op", None, None, None),
            P("tm", None, "op", None),
            P(),
        ),
        out_specs=P("tm", None, "op", None),
        check_vma=False,
    )
```

```python
import jax
import jax.numpy as jnp
from jax import lax
from jax.experimental import pallas as pl
from jax.experimental.pallas import tpu as pltpu
from jax.sharding import PartitionSpec as P

MESH = pl.DeviceIdType.MESH
BF = jnp.bfloat16
F32 = jnp.float32
GROUPS = 3
STRIDE_T = 136
STRIDE_S = 48

HOPS = (
    ((0, 0), (0, 0)),
    ((1, 0), (1, 0)),
    ((3, 0), (3, 0)),
    ((0, 1), (0, 1)),
    ((0, 3), (0, 3)),
    ((3, 3), (1, 1)),
    ((1, 3), (3, 1)),
    ((2, 0), (0, 2)),
)


def dot_t(a, b):
    return lax.dot_general(a, b, (((1,), (1,)), ((), ())), preferred_element_type=F32)


def kernel(
    peram_ref, sink_ref, src_ref, lab_ref, out_ref,
    per_v, sink_v, src_v, lab_v, left, bar, tout, recv, sring, fs, ft, lhs, sw, oret, ogot,
    in_sem, sink_sem, s1_send, s1_recv, ring_send, ring_recv, t_send, t_recv, o_send, o_recv, answer,
):
    tm = lax.axis_index("tm")
    op = lax.axis_index("op")
    core = tm % 2
    x = (tm // 2) % 4
    y = op // 2
    z = (op % 2) * 4 + tm // 8

    def dev(x_, y_, z_, c_):
        return ((z_ % 4) * 8 + x_ * 2 + c_, y_ * 2 + z_ // 4)

    xs4 = [x] + [lax.rem(x + d, 4) for d in range(1, 4)]
    ys4 = [y] + [lax.rem(y + d, 4) for d in range(1, 4)]
    first_tm = tm // 8 * 8
    z_hi = op % 2

    def near(x_, y_, c_):
        return (first_tm + x_ * 2 + c_, y_ * 2 + z_hi)

    def block_of(x_, y_):
        p = lax.rem(x_ + 4 - y_, 4)
        r = lax.rem(p, 2)
        return lax.rem(y_, 2) + p - r, r

    my_ys, my_r = block_of(x, y)
    other_core = near(x, y, 1 - core)
    sends = {}
    owners = {}
    for cls in range(1, 8):
        for lh in range(2):
            dx, dy = HOPS[cls][lh]
            sends[cls, lh] = near(xs4[dx], ys4[dy], lh), block_of(xs4[dx], ys4[dy])
        (dx0, dy0), (dx1, dy1) = HOPS[cls]
        x0, y0, x1, y1 = xs4[-dx0 % 4], ys4[-dy0 % 4], xs4[-dx1 % 4], ys4[-dy1 % 4]
        xo, yo = x0 + core * (x1 - x0), y0 + core * (y1 - y0)
        for cs in range(2):
            owners[cls, cs] = near(xo, yo, cs)

    cp_src = pltpu.make_async_copy(src_ref, src_v, in_sem.at[0])
    cp_per = pltpu.make_async_copy(peram_ref.at[0], per_v, in_sem.at[1])
    cp_lab = pltpu.make_async_copy(lab_ref, lab_v, in_sem.at[2])
    cp_src.start()
    cp_per.start()
    cp_lab.start()
    cp_sink = [
        pltpu.make_async_copy(sink_ref.at[0, pl.ds(4 * g, 4)], sink_v.at[pl.ds(4 * g, 4)], sink_sem.at[g])
        for g in range(GROUPS)
    ]
    for cp in cp_sink:
        cp.start()

    barrier = pltpu.get_barrier_semaphore()

    for y_n in ys4:
        for x_n in xs4:
            for c_n in (1 - core, core):
                if not (x_n is x and y_n is y and c_n is core):
                    pl.semaphore_signal(barrier, inc=1, device_id=near(x_n, y_n, c_n), device_id_type=MESH)

    z_up = (z + 1) % 8
    z_dn = (z + 7) % 8
    above = dev(x, y, z_up, core)
    below = dev(x, y, z_dn, core)
    later_up = z < 7
    later_dn = z == 0
    for z_n, later in ((z_up, later_up), (z_dn, later_dn)):
        @pl.when(later)
        def _():
            pl.semaphore_signal(barrier, inc=1, device_id=above if z_n is z_up else below, device_id_type=MESH)

    def turned(g):
        cp_sink[g].wait()
        prods = []
        for i4 in range(4):
            i = 4 * g + i4
            elem = jnp.concatenate([sink_v[i, 0], sink_v[i, 1]], axis=1)
            prod = dot_t(left[...], elem).astype(BF)
            prods.append(jnp.concatenate([prod[0:256], prod[256:512]], axis=1))
        for i4 in range(4):
            turn = jnp.dot(prods[i4], bar[...], preferred_element_type=F32).astype(BF)
            for ys in range(4):
                for h in range(2):
                    for r in range(2):
                        b0 = ys * 64 + h * 32 + r * 16
                        for c in range(2):
                            for lh in range(2):
                                tout[ys, r, lh, g, c * 4 + i4, h] = turn[
                                    b0:b0 + 16, c * 256 + lh * 128:c * 256 + lh * 128 + 128
                                ]

    cp_src.wait()
    pl.semaphore_wait(barrier, 31 + jnp.where(z > 0, 1, 0) + jnp.where(z == 7, 1, 0))
    for z_n, later, at in ((z_up, later_up, 1), (z_dn, later_dn, 0)):
        @pl.when(jnp.logical_not(later))
        def _():
            pl.semaphore_signal(answer.at[at], inc=1, device_id=above if z_n is z_up else below, device_id_type=MESH)

    first = []
    for r in range(2):
        for far in range(2):
            xd = lax.rem(2 * y - lax.rem(y, 2) + r + 2 * far, 4)
            yd = ys4[2 * far]
            for lh in range(2):
                src = src_v.at[:, :, pl.ds(16 * r, 16), pl.ds(128 * lh, 128)]
                me8 = lax.rem(x + 4 - xd, 4) * 2 + core
                dst = sring.at[0, me8]
                k = (r * 2 + far) * 2 + lh
                cp = pltpu.make_async_remote_copy(
                    src, dst, s1_send.at[k], s1_recv.at[me8],
                    device_id=near(xd, yd, lh), device_id_type=MESH,
                )
                if far:
                    cp.start()
                    first.append((cp, None))
                else:
                    mine = jnp.logical_and(xd == x, core == lh)

                    @pl.when(jnp.logical_not(mine))
                    def _():
                        cp.start()

                    @pl.when(mine)
                    def _():
                        pltpu.make_async_copy(src, dst, s1_recv.at[me8]).start()

                    first.append((cp, jnp.logical_not(mine)))

    def ring(slot_from, slot_to, z_n, ch):
        return pltpu.make_async_remote_copy(
            sring.at[slot_from, pl.ds(2 * ch, 2)], sring.at[slot_to, pl.ds(2 * ch, 2)],
            ring_send.at[slot_from, ch] if z_n is z_up else ring_send.at[8 + slot_from, ch],
            ring_recv.at[slot_to, ch],
            device_id=above if z_n is z_up else below, device_id_type=MESH,
        )

    ring_cps = []

    def ring_up(k, ch):
        ring_wait(k - 1, ch)
        cp = ring(k - 1, k, z_up, ch)
        cp.start()
        ring_cps.append(cp)

    def ring_down(k, ch, cond=None):
        ring_wait((9 - k) % 8, ch)
        cp = ring((9 - k) % 8, 8 - k, z_dn, ch)
        if cond is None:
            cp.start()
        else:
            pl.when(cond)(cp.start)
        return cp

    def ring_step(k, ch):
        ring_cps.append(ring_down(k, ch))
        if k < 4:
            ring_up(k, ch)

    waited = set()

    def ring_wait(slot, ch):
        if (slot, ch) in waited:
            return
        waited.add((slot, ch))
        if slot == 0:
            for k in (2 * ch, 2 * ch + 1):
                ref = sring.at[0, k]
                pltpu.make_async_copy(ref, ref, s1_recv.at[k]).wait()
            return
        ref = sring.at[slot, pl.ds(2 * ch, 2)]
        pltpu.make_async_copy(ref, ref, ring_recv.at[slot, ch]).wait()

    def place_source(d):
        zs = (z + 8 - d) % 8
        h = zs // 4
        zl = zs % 4

        @pl.loop(0, 4)
        def _(ch):
            xs = (x + ch) % 4
            for cs in range(2):
                for j in range(3):
                    for c in range(2):
                        tile = sring[d, 2 * ch + cs, j, c].astype(F32)
                        fs[h, zl, pl.ds(xs * 6 + c * 24 + cs * 3 + j, 16, STRIDE_S), :] = tile

    t_cps = []

    def send_turned(g):
        for cls in (0, 1, 2, 3, 4, 7, 5, 6):
            if cls == 0:
                cp = pltpu.make_async_remote_copy(
                    tout.at[my_ys, my_r, 1 - core, g], recv.at[core, g],
                    t_send.at[g, 0], t_recv.at[core, g],
                    device_id=other_core, device_id_type=MESH,
                )
                cp.start()
                t_cps.append(cp)
                pltpu.make_async_copy(tout.at[my_ys, my_r, core, g], recv.at[core, g], t_recv.at[core, g]).start()
                continue
            for lh in range(2):
                target, (ys, r) = sends[cls, lh]
                cp = pltpu.make_async_remote_copy(
                    tout.at[ys, r, lh, g], recv.at[2 * cls + core, g],
                    t_send.at[g, 2 * cls + lh], t_recv.at[2 * cls + core, g],
                    device_id=target, device_id_type=MESH,
                )
                cp.start()
                t_cps.append(cp)

    def gather_rows(g):
        @pl.loop(0, 8)
        def _(k):
            cls = k
            for cs in range(2):
                ref = recv.at[2 * cls + cs, g]
                pltpu.make_async_copy(ref, ref, t_recv.at[2 * cls + cs, g]).wait()
                for ci in range(8):
                    for h in range(2):
                        tile = recv[2 * cls + cs, g, ci, h].astype(F32)
                        ft[h, pl.ds(cls * 16 + cs * 8 + ci, 16, STRIDE_T), :] = tile
            for b in range(16):
                for h in range(2):
                    tile = ft[h, pl.ds(b * STRIDE_T + cls * 16, 16), :]
                    lhs[b, pl.ds(g * 128 + cls * 16, 16), h * 128:h * 128 + 128] = tile.astype(BF)

    cp_per.wait()
    pr = per_v[0].astype(F32)
    pi = per_v[1].astype(F32)
    prt = pr.T.astype(BF)
    pit = pi.T
    left[0:256, 0:256] = prt
    left[256:512, 256:512] = prt
    left[256:512, 0:256] = pit.astype(BF)
    left[0:256, 256:512] = (-pit).astype(BF)
    row = lax.broadcasted_iota(jnp.int32, (256, 256), 0) < 128
    col = lax.broadcasted_iota(jnp.int32, (256, 256), 1) < 128
    flip = jnp.where(row == col, 1.0, -1.0).astype(F32)
    br = (pr * flip).astype(BF)
    bi = -(pi * flip)
    bar[0:256, 0:256] = br
    bar[256:512, 256:512] = br
    bar[0:256, 256:512] = bi.astype(BF)
    bar[256:512, 0:256] = (-bi).astype(BF)

    turned(0)
    send_turned(0)
    turned(1)

    @pl.when(later_up)
    def _():
        pl.semaphore_wait(answer.at[0], 1)

    for ch in range(4):
        ring_up(1, ch)
        ring_cps.append(ring_down(1, ch, jnp.logical_not(later_dn)))
        if ch == 1:
            send_turned(1)
    turned(2)
    send_turned(2)

    @pl.when(later_dn)
    def _():
        pl.semaphore_wait(answer.at[1], 1)
        for ch in range(4):
            ring(0, 7, z_dn, ch).start()

    place_source(0)
    ring_step(2, 0)
    ring_step(2, 1)
    ring_step(2, 2)
    ring_step(2, 3)
    place_source(1)
    place_source(7)
    for ch in range(4):
        ring_step(3, ch)
    place_source(2)
    place_source(6)
    gather_rows(0)
    for ch in range(4):
        ring_step(4, ch)
    gather_rows(1)
    for slot in (5, 3, 4):
        if slot == 4:
            gather_rows(2)
        for ch in range(4):
            ring_wait(slot, ch)
        place_source(slot)

    cp_lab.wait()
    labels = jnp.broadcast_to(lab_v[...].astype(F32), (8, 96))
    lane = lax.broadcasted_iota(jnp.int32, (8, 96), 1)
    sub = lax.broadcasted_iota(jnp.int32, (8, 96), 0) % 4
    same = []
    for g in range(GROUPS):
        own = jnp.sum(jnp.where(lane == op * 12 + 4 * g + sub, labels, 0.0), axis=1, keepdims=True)
        same.append((own == labels).astype(F32))

    o_cps = []

    @pl.loop(0, 16, unroll=2)
    def _(b):
        for h in range(2):
            for c in range(2):
                rows = [fs[h, zl, pl.ds(b * STRIDE_S + c * 24, 24), :] for zl in range(4)]
                if c == 0:
                    rows.append(jnp.zeros((32, 128), F32))
                rows = jnp.concatenate(rows, axis=0).astype(BF)
                sw[b, c * 128:c * 128 + rows.shape[0], h * 128:h * 128 + 128] = rows

    acc = dot_t(lhs[0], sw[0])
    for b in range(1, 16):
        acc = acc + dot_t(lhs[b], sw[b])
    with_re = acc[:, 0:128].reshape(48, 8, 128)
    with_im = jnp.concatenate([acc[:, 128:224], jnp.zeros((384, 32), F32)], axis=1).reshape(48, 8, 128)
    with_im = jnp.concatenate([with_im[:, 4:8], with_im[:, 0:4]], axis=1)
    sign = jnp.where(lax.broadcasted_iota(jnp.int32, (48, 8, 128), 1) < 4, -1.0, 1.0).astype(F32)
    oret[...] = (with_re + sign * with_im).reshape(3, 16, 8, 128)

    for cls in (7, 6, 5, 4, 3, 2, 1, 0):
        if cls == 0:
            cp = pltpu.make_async_remote_copy(
                oret.at[:, 1 - core], ogot.at[:, core], o_send.at[0], o_recv.at[core],
                device_id=other_core, device_id_type=MESH,
            )
            cp.start()
            o_cps.append(cp)
            continue
        for cs in range(2):
            cp = pltpu.make_async_remote_copy(
                oret.at[:, 2 * cls + cs], ogot.at[:, 2 * cls + core],
                o_send.at[2 * cls + cs], o_recv.at[2 * cls + core],
                device_id=owners[cls, cs], device_id_type=MESH,
            )
            cp.start()
            o_cps.append(cp)

    total = oret[:, core]
    ref = ogot.at[:, 1 - core]
    pltpu.make_async_copy(ref, ref, o_recv.at[1 - core]).wait()
    total = total + ogot[:, 1 - core]
    for slot in range(2, 16):
        ref = ogot.at[:, slot]
        pltpu.make_async_copy(ref, ref, o_recv.at[slot]).wait()
        total = total + ogot[:, slot]
    for g in range(GROUPS):
        out = total[g, :, 0:96] * same[g]
        for c in range(2):
            for i4 in range(4):
                out_ref[4 * g + i4, c:c + 1, :] = out[4 * c + i4:4 * c + i4 + 1, :]

    for cp, cond in first:
        if cond is None:
            cp.wait_send()
        else:
            @pl.when(cond)
            def _():
                cp.wait_send()
    for cp in ring_cps + t_cps + o_cps:
        cp.wait_send()


def local(peram, sink_elementals, source_elementals, irrep):
    dma = pltpu.SemaphoreType.DMA
    full = pl.pallas_call(
        kernel,
        out_shape=jax.ShapeDtypeStruct((12, 2, 96), F32),
        in_specs=[pl.BlockSpec(memory_space=pl.ANY)] * 4,
        out_specs=pl.BlockSpec(memory_space=pltpu.VMEM),
        scratch_shapes=[
            pltpu.VMEM((2, 256, 256), BF),
            pltpu.VMEM((12, 2, 256, 256), BF),
            pltpu.VMEM((3, 2, 32, 256), BF),
            pltpu.VMEM((1, 96), jnp.int32),
            pltpu.VMEM((512, 512), BF),
            pltpu.VMEM((512, 512), BF),
            pltpu.VMEM((4, 2, 2, 3, 8, 2, 16, 128), BF),
            pltpu.VMEM((16, 3, 8, 2, 16, 128), BF),
            pltpu.VMEM((8, 8, 3, 2, 16, 128), BF),
            pltpu.VMEM((2, 4, 16 * STRIDE_S, 128), F32),
            pltpu.VMEM((2, 16 * STRIDE_T, 128), F32),
            pltpu.VMEM((16, 384, 256), BF),
            pltpu.VMEM((16, 224, 256), BF),
            pltpu.VMEM((3, 16, 8, 128), F32),
            pltpu.VMEM((3, 16, 8, 128), F32),
            dma((3,)),
            dma((3,)),
            dma((8,)),
            dma((8,)),
            dma((16, 4)),
            dma((8, 4)),
            dma((3, 16)),
            dma((16, 3)),
            dma((16,)),
            dma((16,)),
            pltpu.SemaphoreType.REGULAR((2,)),
        ],
        compiler_params=pltpu.CompilerParams(
            collective_id=0, has_side_effects=True, vmem_limit_bytes=60 * 1024 * 1024
        ),
        cost_estimate=pl.CostEstimate(flops=7_000_000_000, bytes_accessed=4_000_000, transcendentals=0),
    )(peram, sink_elementals, source_elementals, irrep.reshape(1, 96))
    return jnp.swapaxes(full, 0, 1)[None]


def solution(mesh):
    return jax.shard_map(
        local,
        mesh=mesh,
        in_specs=(
            P("tm", None, None, None),
            P("tm", "op", None, None, None),
            P("tm", None, "op", None),
            P(),
        ),
        out_specs=P("tm", None, "op", None),
        check_vma=False,
    )
```

```python
import jax
import jax.numpy as jnp
from jax import lax
from jax.experimental import pallas as pl
from jax.experimental.pallas import tpu as pltpu
from jax.sharding import PartitionSpec as P

MESH = pl.DeviceIdType.MESH
BF = jnp.bfloat16
F32 = jnp.float32
GROUPS = 3
STRIDE_T = 136
STRIDE_S = 48

HOPS = (
    ((0, 0), (0, 0)),
    ((1, 0), (1, 0)),
    ((3, 0), (3, 0)),
    ((0, 1), (0, 1)),
    ((0, 3), (0, 3)),
    ((3, 3), (1, 1)),
    ((1, 3), (3, 1)),
    ((2, 0), (0, 2)),
)


def dot_t(a, b):
    return lax.dot_general(a, b, (((1,), (1,)), ((), ())), preferred_element_type=F32)


def kernel(
    peram_ref, sink_ref, src_ref, lab_ref, out_ref,
    per_v, sink_v, src_v, lab_v, left, bar, tout, recv, sring, fs, ft, lhs, sw, oret, ogot,
    in_sem, sink_sem, s1_send, s1_recv, ring_send, ring_recv, t_send, t_recv, o_send, o_recv, answer,
):
    tm = lax.axis_index("tm")
    op = lax.axis_index("op")
    core = tm % 2
    x = (tm // 2) % 4
    y = op // 2
    z = (op % 2) * 4 + tm // 8

    def dev(x_, y_, z_, c_):
        return ((z_ % 4) * 8 + x_ * 2 + c_, y_ * 2 + z_ // 4)

    xs4 = [x] + [lax.rem(x + d, 4) for d in range(1, 4)]
    ys4 = [y] + [lax.rem(y + d, 4) for d in range(1, 4)]
    first_tm = tm // 8 * 8
    z_hi = op % 2

    def near(x_, y_, c_):
        return (first_tm + x_ * 2 + c_, y_ * 2 + z_hi)

    def block_of(x_, y_):
        p = lax.rem(x_ + 4 - y_, 4)
        r = lax.rem(p, 2)
        return lax.rem(y_, 2) + p - r, r

    my_ys, my_r = block_of(x, y)
    other_core = near(x, y, 1 - core)
    sends = {}
    owners = {}
    for cls in range(1, 8):
        for lh in range(2):
            dx, dy = HOPS[cls][lh]
            sends[cls, lh] = near(xs4[dx], ys4[dy], lh), block_of(xs4[dx], ys4[dy])
        (dx0, dy0), (dx1, dy1) = HOPS[cls]
        x0, y0, x1, y1 = xs4[-dx0 % 4], ys4[-dy0 % 4], xs4[-dx1 % 4], ys4[-dy1 % 4]
        xo, yo = x0 + core * (x1 - x0), y0 + core * (y1 - y0)
        for cs in range(2):
            owners[cls, cs] = near(xo, yo, cs)

    cp_src = pltpu.make_async_copy(src_ref, src_v, in_sem.at[0])
    cp_per = pltpu.make_async_copy(peram_ref.at[0], per_v, in_sem.at[1])
    cp_lab = pltpu.make_async_copy(lab_ref, lab_v, in_sem.at[2])
    cp_src.start()
    cp_per.start()
    cp_lab.start()
    cp_sink = [
        pltpu.make_async_copy(sink_ref.at[0, pl.ds(4 * g, 4)], sink_v.at[pl.ds(4 * g, 4)], sink_sem.at[g])
        for g in range(GROUPS)
    ]
    for cp in cp_sink:
        cp.start()

    barrier = pltpu.get_barrier_semaphore()

    for y_n in ys4:
        for x_n in xs4:
            for c_n in (1 - core, core):
                if not (x_n is x and y_n is y and c_n is core):
                    pl.semaphore_signal(barrier, inc=1, device_id=near(x_n, y_n, c_n), device_id_type=MESH)

    z_up = (z + 1) % 8
    z_dn = (z + 7) % 8
    above = dev(x, y, z_up, core)
    below = dev(x, y, z_dn, core)
    later_up = z < 7
    later_dn = z == 0
    for z_n, later in ((z_up, later_up), (z_dn, later_dn)):
        @pl.when(later)
        def _():
            pl.semaphore_signal(barrier, inc=1, device_id=above if z_n is z_up else below, device_id_type=MESH)

    def turned(g):
        cp_sink[g].wait()
        prods = []
        for i4 in range(4):
            i = 4 * g + i4
            elem = jnp.concatenate([sink_v[i, 0], sink_v[i, 1]], axis=1)
            prod = dot_t(left[...], elem).astype(BF)
            prods.append(jnp.concatenate([prod[0:256], prod[256:512]], axis=1))
        for i4 in range(4):
            turn = jnp.dot(prods[i4], bar[...], preferred_element_type=F32).astype(BF)
            for ys in range(4):
                for h in range(2):
                    for r in range(2):
                        b0 = ys * 64 + h * 32 + r * 16
                        for c in range(2):
                            for lh in range(2):
                                tout[ys, r, lh, g, c * 4 + i4, h] = turn[
                                    b0:b0 + 16, c * 256 + lh * 128:c * 256 + lh * 128 + 128
                                ]

    cp_src.wait()
    pl.semaphore_wait(barrier, 31 + jnp.where(z > 0, 1, 0) + jnp.where(z == 7, 1, 0))
    for z_n, later, at in ((z_up, later_up, 1), (z_dn, later_dn, 0)):
        @pl.when(jnp.logical_not(later))
        def _():
            pl.semaphore_signal(answer.at[at], inc=1, device_id=above if z_n is z_up else below, device_id_type=MESH)

    first = []
    for r in range(2):
        for far in range(2):
            xd = lax.rem(2 * y - lax.rem(y, 2) + r + 2 * far, 4)
            yd = ys4[2 * far]
            for lh in range(2):
                src = src_v.at[:, :, pl.ds(16 * r, 16), pl.ds(128 * lh, 128)]
                me8 = lax.rem(x + 4 - xd, 4) * 2 + core
                dst = sring.at[0, me8]
                k = (r * 2 + far) * 2 + lh
                cp = pltpu.make_async_remote_copy(
                    src, dst, s1_send.at[k], s1_recv.at[me8],
                    device_id=near(xd, yd, lh), device_id_type=MESH,
                )
                if far:
                    cp.start()
                    first.append((cp, None))
                else:
                    mine = jnp.logical_and(xd == x, core == lh)

                    @pl.when(jnp.logical_not(mine))
                    def _():
                        cp.start()

                    @pl.when(mine)
                    def _():
                        pltpu.make_async_copy(src, dst, s1_recv.at[me8]).start()

                    first.append((cp, jnp.logical_not(mine)))

    def ring(slot_from, slot_to, z_n, ch):
        return pltpu.make_async_remote_copy(
            sring.at[slot_from, pl.ds(2 * ch, 2)], sring.at[slot_to, pl.ds(2 * ch, 2)],
            ring_send.at[slot_from, ch] if z_n is z_up else ring_send.at[8 + slot_from, ch],
            ring_recv.at[slot_to, ch],
            device_id=above if z_n is z_up else below, device_id_type=MESH,
        )

    ring_cps = []

    def ring_up(k, ch):
        ring_wait(k - 1, ch)
        cp = ring(k - 1, k, z_up, ch)
        cp.start()
        ring_cps.append(cp)

    def ring_down(k, ch, cond=None):
        ring_wait((9 - k) % 8, ch)
        cp = ring((9 - k) % 8, 8 - k, z_dn, ch)
        if cond is None:
            cp.start()
        else:
            pl.when(cond)(cp.start)
        return cp

    def ring_step(k, ch):
        ring_cps.append(ring_down(k, ch))
        if k < 4:
            ring_up(k, ch)

    waited = set()

    def ring_wait(slot, ch):
        if (slot, ch) in waited:
            return
        waited.add((slot, ch))
        if slot == 0:
            for k in (2 * ch, 2 * ch + 1):
                ref = sring.at[0, k]
                pltpu.make_async_copy(ref, ref, s1_recv.at[k]).wait()
            return
        ref = sring.at[slot, pl.ds(2 * ch, 2)]
        pltpu.make_async_copy(ref, ref, ring_recv.at[slot, ch]).wait()

    def place_source(d):
        zs = (z + 8 - d) % 8
        h = zs // 4
        zl = zs % 4

        @pl.loop(0, 4)
        def _(ch):
            xs = (x + ch) % 4
            for cs in range(2):
                for j in range(3):
                    for c in range(2):
                        tile = sring[d, 2 * ch + cs, j, c].astype(F32)
                        fs[h, zl, pl.ds(xs * 6 + c * 24 + cs * 3 + j, 16, STRIDE_S), :] = tile

    t_cps = []

    def send_turned(g):
        for cls in (0, 1, 2, 3, 4, 7, 5, 6):
            if cls == 0:
                cp = pltpu.make_async_remote_copy(
                    tout.at[my_ys, my_r, 1 - core, g], recv.at[core, g],
                    t_send.at[g, 0], t_recv.at[core, g],
                    device_id=other_core, device_id_type=MESH,
                )
                cp.start()
                t_cps.append(cp)
                pltpu.make_async_copy(tout.at[my_ys, my_r, core, g], recv.at[core, g], t_recv.at[core, g]).start()
                continue
            for lh in range(2):
                target, (ys, r) = sends[cls, lh]
                cp = pltpu.make_async_remote_copy(
                    tout.at[ys, r, lh, g], recv.at[2 * cls + core, g],
                    t_send.at[g, 2 * cls + lh], t_recv.at[2 * cls + core, g],
                    device_id=target, device_id_type=MESH,
                )
                cp.start()
                t_cps.append(cp)

    def gather_rows(g):
        @pl.loop(0, 8)
        def _(k):
            cls = k
            for cs in range(2):
                ref = recv.at[2 * cls + cs, g]
                pltpu.make_async_copy(ref, ref, t_recv.at[2 * cls + cs, g]).wait()
                for ci in range(8):
                    for h in range(2):
                        tile = recv[2 * cls + cs, g, ci, h].astype(F32)
                        ft[h, pl.ds(cls * 16 + cs * 8 + ci, 16, STRIDE_T), :] = tile
            for b in range(16):
                for h in range(2):
                    tile = ft[h, pl.ds(b * STRIDE_T + cls * 16, 16), :]
                    lhs[b, pl.ds(g * 128 + cls * 16, 16), h * 128:h * 128 + 128] = tile.astype(BF)

    cp_per.wait()
    pr = per_v[0].astype(F32)
    pi = per_v[1].astype(F32)
    prt = pr.T.astype(BF)
    pit = pi.T
    left[0:256, 0:256] = prt
    left[256:512, 256:512] = prt
    left[256:512, 0:256] = pit.astype(BF)
    left[0:256, 256:512] = (-pit).astype(BF)
    row = lax.broadcasted_iota(jnp.int32, (256, 256), 0) < 128
    col = lax.broadcasted_iota(jnp.int32, (256, 256), 1) < 128
    flip = jnp.where(row == col, 1.0, -1.0).astype(F32)
    br = (pr * flip).astype(BF)
    bi = -(pi * flip)
    bar[0:256, 0:256] = br
    bar[256:512, 256:512] = br
    bar[0:256, 256:512] = bi.astype(BF)
    bar[256:512, 0:256] = (-bi).astype(BF)

    turned(0)
    send_turned(0)
    turned(1)

    @pl.when(later_up)
    def _():
        pl.semaphore_wait(answer.at[0], 1)

    for ch in range(4):
        ring_up(1, ch)
        ring_cps.append(ring_down(1, ch, jnp.logical_not(later_dn)))
        if ch == 1:
            send_turned(1)
    turned(2)
    send_turned(2)

    @pl.when(later_dn)
    def _():
        pl.semaphore_wait(answer.at[1], 1)
        for ch in range(4):
            ring(0, 7, z_dn, ch).start()

    place_source(0)
    ring_step(2, 0)
    ring_step(2, 1)
    ring_step(2, 2)
    ring_step(2, 3)
    place_source(1)
    place_source(7)
    for ch in range(4):
        ring_step(3, ch)
    place_source(2)
    place_source(6)
    cp_lab.wait()
    labels = jnp.broadcast_to(lab_v[...].astype(F32), (8, 96))
    lane = lax.broadcasted_iota(jnp.int32, (8, 96), 1)
    sub = lax.broadcasted_iota(jnp.int32, (8, 96), 0) % 4
    same = []
    for g in range(GROUPS):
        own = jnp.sum(jnp.where(lane == op * 12 + 4 * g + sub, labels, 0.0), axis=1, keepdims=True)
        same.append((own == labels).astype(F32))

    gather_rows(0)
    for ch in range(4):
        ring_step(4, ch)
    gather_rows(1)
    for slot in (5, 3, 4):
        if slot == 4:
            gather_rows(2)
        for ch in range(4):
            ring_wait(slot, ch)
        place_source(slot)

    o_cps = []

    @pl.loop(0, 16, unroll=2)
    def _(b):
        for h in range(2):
            for c in range(2):
                rows = [fs[h, zl, pl.ds(b * STRIDE_S + c * 24, 24), :] for zl in range(4)]
                if c == 0:
                    rows.append(jnp.zeros((32, 128), F32))
                rows = jnp.concatenate(rows, axis=0).astype(BF)
                sw[b, c * 128:c * 128 + rows.shape[0], h * 128:h * 128 + 128] = rows

    acc = dot_t(lhs[0], sw[0])
    for b in range(1, 16):
        acc = acc + dot_t(lhs[b], sw[b])
    with_re = acc[:, 0:128].reshape(48, 8, 128)
    with_im = jnp.concatenate([acc[:, 128:224], jnp.zeros((384, 32), F32)], axis=1).reshape(48, 8, 128)
    with_im = jnp.concatenate([with_im[:, 4:8], with_im[:, 0:4]], axis=1)
    sign = jnp.where(lax.broadcasted_iota(jnp.int32, (48, 8, 128), 1) < 4, -1.0, 1.0).astype(F32)
    oret[...] = (with_re + sign * with_im).reshape(3, 16, 8, 128)

    for cls in (7, 6, 5, 4, 3, 2, 1, 0):
        if cls == 0:
            cp = pltpu.make_async_remote_copy(
                oret.at[:, 1 - core], ogot.at[:, core], o_send.at[0], o_recv.at[core],
                device_id=other_core, device_id_type=MESH,
            )
            cp.start()
            o_cps.append(cp)
            continue
        for cs in range(2):
            cp = pltpu.make_async_remote_copy(
                oret.at[:, 2 * cls + cs], ogot.at[:, 2 * cls + core],
                o_send.at[2 * cls + cs], o_recv.at[2 * cls + core],
                device_id=owners[cls, cs], device_id_type=MESH,
            )
            cp.start()
            o_cps.append(cp)

    total = oret[:, core]
    ref = ogot.at[:, 1 - core]
    pltpu.make_async_copy(ref, ref, o_recv.at[1 - core]).wait()
    total = total + ogot[:, 1 - core]
    for slot in range(2, 16):
        ref = ogot.at[:, slot]
        pltpu.make_async_copy(ref, ref, o_recv.at[slot]).wait()
        total = total + ogot[:, slot]
    for g in range(GROUPS):
        out = total[g, :, 0:96] * same[g]
        for c in range(2):
            for i4 in range(4):
                out_ref[4 * g + i4, c:c + 1, :] = out[4 * c + i4:4 * c + i4 + 1, :]

    for cp, cond in first:
        if cond is None:
            cp.wait_send()
        else:
            @pl.when(cond)
            def _():
                cp.wait_send()
    for cp in ring_cps + t_cps + o_cps:
        cp.wait_send()


def local(peram, sink_elementals, source_elementals, irrep):
    dma = pltpu.SemaphoreType.DMA
    full = pl.pallas_call(
        kernel,
        out_shape=jax.ShapeDtypeStruct((12, 2, 96), F32),
        in_specs=[pl.BlockSpec(memory_space=pl.ANY)] * 4,
        out_specs=pl.BlockSpec(memory_space=pltpu.VMEM),
        scratch_shapes=[
            pltpu.VMEM((2, 256, 256), BF),
            pltpu.VMEM((12, 2, 256, 256), BF),
            pltpu.VMEM((3, 2, 32, 256), BF),
            pltpu.VMEM((1, 96), jnp.int32),
            pltpu.VMEM((512, 512), BF),
            pltpu.VMEM((512, 512), BF),
            pltpu.VMEM((4, 2, 2, 3, 8, 2, 16, 128), BF),
            pltpu.VMEM((16, 3, 8, 2, 16, 128), BF),
            pltpu.VMEM((8, 8, 3, 2, 16, 128), BF),
            pltpu.VMEM((2, 4, 16 * STRIDE_S, 128), F32),
            pltpu.VMEM((2, 16 * STRIDE_T, 128), F32),
            pltpu.VMEM((16, 384, 256), BF),
            pltpu.VMEM((16, 224, 256), BF),
            pltpu.VMEM((3, 16, 8, 128), F32),
            pltpu.VMEM((3, 16, 8, 128), F32),
            dma((3,)),
            dma((3,)),
            dma((8,)),
            dma((8,)),
            dma((16, 4)),
            dma((8, 4)),
            dma((3, 16)),
            dma((16, 3)),
            dma((16,)),
            dma((16,)),
            pltpu.SemaphoreType.REGULAR((2,)),
        ],
        compiler_params=pltpu.CompilerParams(
            collective_id=0, has_side_effects=True, vmem_limit_bytes=60 * 1024 * 1024
        ),
        cost_estimate=pl.CostEstimate(flops=7_000_000_000, bytes_accessed=4_000_000, transcendentals=0),
    )(peram, sink_elementals, source_elementals, irrep.reshape(1, 96))
    return jnp.swapaxes(full, 0, 1)[None]


def solution(mesh):
    return jax.shard_map(
        local,
        mesh=mesh,
        in_specs=(
            P("tm", None, None, None),
            P("tm", "op", None, None, None),
            P("tm", None, "op", None),
            P(),
        ),
        out_specs=P("tm", None, "op", None),
        check_vma=False,
    )
```
